32 devices in a mesh: tm: 16 (over z, y, x), chan: 2 (over core).
Axes of the slice: x: 2, y: 2, z: 4, core: 2. Of those that a mesh axis runs over, the one named last changes fastest.
Arguments:
- latents: bfloat16 [96, 32, 896], P('chan', 'tm'), may hold values from -6 to 6
- weight: bfloat16 [27, 96, 96], replicated, may hold values from -0.125 to 0.125
- conv_bias: bfloat16 [96], P('chan'), may hold values from -3 to 3
- cotangent: bfloat16 [96, 32, 896], P('chan', 'tm'), may hold values from -6 to 6
Outputs:
- output: bfloat16 [96, 32, 896], P('chan', 'tm')
- grad_input: bfloat16 [96, 32, 896], P('chan', 'tm')
- grad_weight: float32 [27, 96, 96], P(None, 'chan')
- grad_bias: float32 [96], P('chan')
The draws below stay inside these ranges and needn't reach their ends.
All inputs are finite; a program needn't handle non-finite values.
Results may differ from the reference program's by a relative error of at most 0.0085.
Values may be sent and summed in bfloat16 or wider, within the bound.
A program may use at most 64 MiB of HBM per device.

```python
import math
import jax
import jax.numpy as jnp
from jax import lax

CH = 96
HGT = 8
WID = 112
NF = 32
PIX = 896


def shard_levels(own_key, dims, pieces, smallest, largest):
    factor_of, own = 1.0, jax.random.fold_in(own_key, 6)
    for dim, parts in pieces:
        steps = jnp.exp(jax.random.uniform(jax.random.fold_in(own, dim), (parts,), jnp.float32, smallest / len(pieces), largest / len(pieces)))
        factor_of = factor_of * jnp.repeat(steps, dims[dim] // parts).reshape([-1 if axis == dim else 1 for axis in range(len(dims))])
    return factor_of


def noise(rng, shape, width, bound, cuts=(), held_as=jnp.bfloat16):
    gain = shard_levels(rng, shape, cuts, -0.22, 0.18) if cuts else 1.0
    entries = jax.random.normal(rng, shape, jnp.float32) * width * gain
    return jnp.minimum(jnp.maximum(entries, -bound), bound).astype(held_as)


def setup_inputs(seed: int = 0) -> dict:
    streams_of = jax.random.split(jax.random.key(seed), 5)
    return {
        "latents": noise(streams_of[0], (CH, NF, PIX), 1.0, 6.0, ((0, 2), (1, 16))),
        "weight": noise(streams_of[1], (27, CH, CH), (27 * CH) ** -0.5, 0.125),
        "conv_bias": noise(streams_of[2], (CH,), 0.5, 3.0, ((0, 2),)),
        "cotangent": noise(streams_of[3], (CH, NF, PIX), 1.0, 6.0, ((0, 2), (1, 16))),
    }


def convolve(inputs, kernels_in):
    kernel = kernels_in.reshape(3, 3, 3, CH, CH).transpose(3, 4, 0, 1, 2)
    return lax.conv_general_dilated(inputs, kernel, (1, 1, 1), ((2, 0), (1, 1), (1, 1)), dimension_numbers=('NCDHW', 'OIDHW', 'NCDHW'), precision=lax.Precision.HIGHEST)

def reference(latents, weight, conv_bias, cotangent):
    frames = latents.astype(jnp.float32).reshape(CH, NF, HGT, WID)[None]
    kernels_in = weight.astype(jnp.float32)
    pre_act = convolve(frames, kernels_in)[0].reshape(CH, NF, PIX) + conv_bias.astype(jnp.float32)[:, None, None]
    sigmoid_pre = jax.nn.sigmoid(pre_act)
    output = (pre_act * sigmoid_pre).astype(jnp.bfloat16)
    grad_pre = (cotangent.astype(jnp.float32) * sigmoid_pre * (1.0 + pre_act * (1.0 - sigmoid_pre))).astype(jnp.bfloat16)
    unused, pullback = jax.vjp(convolve, frames, kernels_in)
    grad_in, grad_w = pullback(grad_pre.astype(jnp.float32).reshape(CH, NF, HGT, WID)[None])
    norm_scale = 1.0 / math.sqrt(NF * PIX)
    grad_input = grad_in[0].reshape(CH, NF, PIX).astype(jnp.bfloat16)
    grad_weight = grad_w * norm_scale
    grad_bias = lax.optimization_barrier(jnp.sum(grad_pre.astype(jnp.float32), axis=(1, 2))) * norm_scale
    return (output, grad_input, grad_weight, grad_bias)
```

```python
import functools
import math

import jax
import jax.numpy as jnp
from jax import lax
from jax.experimental import pallas as pl
from jax.experimental.pallas import tpu as pltpu
from jax.sharding import PartitionSpec as P

HGT = 8
WID = 112
MESH = pl.DeviceIdType.MESH
F32 = jnp.float32
BF16 = jnp.bfloat16


def dot(a, b):
    return jnp.dot(a, b, preferred_element_type=F32)


def dot_nt(a, b):
    return lax.dot_general(a, b, (((1,), (1,)), ((), ())), preferred_element_type=F32)


def border_masks(pix):
    place = lax.broadcasted_iota(jnp.int32, (1, pix), 1)
    row = jnp.zeros((1, pix), jnp.int32)
    for k in range(1, HGT):
        row = row + (place >= k * WID).astype(jnp.int32)
    col = place - row * WID
    return (
        (row >= 1).astype(F32),
        (row <= HGT - 2).astype(F32),
        (col >= 1).astype(F32),
        (col <= WID - 2).astype(F32),
    )


def kernel(
    n, scale, norm,
    x_ref, w_ref, b_ref, cot_ref,
    out_ref, gin_ref, gw_ref, gb_ref,
    xe, ge, w_early, w_own, v_own, v_late, y, g9, pack, parts, whole,
    x_send, x_recv, g_send, g_recv, rs_send, rs_recv, ag_send, ag_recv,
):
    own = x_ref.shape[1]
    pix = x_ref.shape[2]
    full = 2 * own
    chunk = pack.shape[0] // n
    me = lax.axis_index("tm")
    ch = lax.axis_index("chan")
    other = 1 - ch
    half = pl.multiple_of(ch * own, 16)
    nxt = lax.rem(me + 1, n)
    prv = lax.rem(me + n - 1, n)

    barrier = pltpu.get_barrier_semaphore()

    def greet(d, carry):
        pl.semaphore_signal(
            barrier, inc=1, device_id=(lax.rem(me + d, n), ch), device_id_type=MESH
        )
        return carry

    pl.semaphore_signal(barrier, inc=1, device_id=(me, other), device_id_type=MESH)
    lax.fori_loop(1, n, greet, 0)

    def rows(frame):
        return pl.ds(pl.multiple_of(frame * full + ch * own, 16), own)

    def copy(buf, src, dst, sems, k, device):
        return pltpu.make_async_remote_copy(
            src_ref=buf.at[rows(src)],
            dst_ref=buf.at[rows(dst)],
            send_sem=sems[0].at[k],
            recv_sem=sems[1].at[k],
            device_id=device,
            device_id_type=MESH,
        )

    xs, gs = (x_send, x_recv), (g_send, g_recv)
    for f in range(2):
        xe[rows(2 + f), :] = x_ref[f]
    pl.semaphore_wait(barrier, n)

    def x_share(f):
        return copy(xe, 2 + f, 2 + f, xs, f, (me, other))

    def x_halo(f):
        return copy(xe, 2 + f, f, xs, 2 + f, (nxt, ch))

    def x_relay(f):
        return copy(xe, f, f, xs, 4 + f, (me, other))

    def g_share(f):
        return copy(ge, f, f, gs, f, (me, other))

    def g_halo(f):
        return copy(ge, f, 2 + f, gs, 2 + f, (prv, ch))

    def g_relay(f):
        return copy(ge, 2 + f, 2 + f, gs, 4 + f, (me, other))

    first, last = me == 0, me == n - 1

    @pl.when(jnp.logical_not(last))
    def _():
        x_halo(1).start()
        x_halo(0).start()

    x_share(0).start()
    x_share(1).start()

    @pl.when(first)
    def _():
        xe[0 : 2 * full, :] = jnp.zeros((2 * full, pix), BF16)

    @pl.when(last)
    def _():
        ge[2 * full : 4 * full, :] = jnp.zeros((2 * full, pix), BF16)

    for tap in range(9):
        to = pl.ds(tap * own, own)
        w0, w1, w2 = (w_ref[9 * t + tap, pl.ds(half, own), :] for t in range(3))
        w_early[to, 0:full] = w0
        w_early[to, full : 2 * full] = w1
        w_own[to, 0:full] = w1
        w_own[to, full : 2 * full] = w2
        v0, v1, v2 = (w_ref[9 * t + tap].T for t in range(3))
        v_own[tap, :, 0:full] = v2
        v_own[tap, :, full : 2 * full] = v1
        v_late[tap, :, 0:full] = v1
        v_late[tap, :, full : 2 * full] = v0

    above, below, left, right = border_masks(pix)

    def spatial_sum(f, block, height, sign):
        def at(kh, kw):
            if sign < 0:
                kh, kw = 2 - kh, 2 - kw
            return y[f, pl.ds((3 * kh + kw) * own + block, height), :]

        z = []
        for kw in range(3):
            z.append(
                at(1, kw)
                + above * pltpu.roll(at(0, kw), WID, 1)
                + below * pltpu.roll(at(2, kw), pix - WID, 1)
            )
        return z[1] + left * pltpu.roll(z[0], 1, 1) + right * pltpu.roll(z[2], pix - 1, 1)

    x_share(0).wait_recv()
    x_share(1).wait_recv()
    taps = 9 * own
    w_last = jnp.concatenate([w_ref[18 + t, pl.ds(half, own), :] for t in range(9)], 0)
    y[0] = dot(w_last, xe[2 * full : 3 * full, :])
    y[1] = dot(w_own[...], xe[2 * full : 4 * full, :])

    @pl.when(jnp.logical_not(first))
    def _():
        for f in (1, 0):
            x_halo(f).wait_recv()
            x_relay(f).start()
        for f in (1, 0):
            x_relay(f).wait_recv()

    bias_sums = []
    for f in (1, 0):
        if f == 1:
            y[1] += dot(w_early[:, 0:full], xe[full : 2 * full, :])
        else:
            y[0] += dot(w_early[...], xe[0 : 2 * full, :])
        sums = []
        for block in range(0, own, 16):
            pre = spatial_sum(f, block, 16, 1) + b_ref[block : block + 16, :].astype(F32)
            sig = jax.nn.sigmoid(pre)
            out_ref[f, block : block + 16, :] = (pre * sig).astype(BF16)
            cot = cot_ref[f, block : block + 16, :].astype(F32)
            grad = (cot * sig * (1.0 + pre * (1.0 - sig))).astype(BF16)
            ge[pl.ds(pl.multiple_of(f * full + ch * own + block, 16), 16), :] = grad
            grad = grad.astype(F32)
            sums.append(jnp.sum(grad, axis=1, keepdims=True))
            moved = (
                right * pltpu.roll(grad, pix - 1, 1),
                grad,
                left * pltpu.roll(grad, 1, 1),
            )
            for kw in range(3):
                shifted = (
                    below * pltpu.roll(moved[kw], pix - WID, 1),
                    moved[kw],
                    above * pltpu.roll(moved[kw], WID, 1),
                )
                for kh in range(3):
                    g9[f, pl.ds((3 * kh + kw) * own + block, 16), :] = shifted[kh].astype(BF16)
        bias_sums.append(jnp.concatenate(sums, 0))
        g_share(f).start()

        @pl.when(jnp.logical_not(first))
        def _():
            g_halo(f).start()

    rest = 3 * full - 256
    piece = 112
    base = 2 * taps
    product = dot_nt(g9[0], xe[0 : 3 * full, :]) + dot_nt(g9[1], xe[full : 4 * full, :])
    pack[0:taps, :] = product[:, 0:128].astype(BF16)
    pack[taps:base, :] = product[:, 128:256].astype(BF16)
    if pack.shape[0] > base:
        pack[base:, :] = jnp.zeros((pack.shape[0] - base, 128), BF16)
    for k in range(4):
        stop = min(taps, (k + 1) * piece)
        pack[base : base + stop - k * piece, rest * k : rest * (k + 1)] = product[
            k * piece : stop, 256 : 256 + rest
        ].astype(BF16)
    lane = lax.broadcasted_iota(jnp.int32, (own, 128), 1)
    pack[base + piece : base + piece + own, :] = jnp.where(
        lane == 0, jnp.broadcast_to(bias_sums[0] + bias_sums[1], (own, 128)), 0.0
    ).astype(BF16)

    def part(i):
        return pl.ds(pl.multiple_of(i * chunk, 16), chunk)

    def rs_copy(d):
        to = lax.rem(me + d, n)
        return pltpu.make_async_remote_copy(
            src_ref=pack.at[part(to)],
            dst_ref=parts.at[d],
            send_sem=rs_send.at[d],
            recv_sem=rs_recv.at[d],
            device_id=(to, ch),
            device_id_type=MESH,
        )

    def ag_copy(d):
        return pltpu.make_async_remote_copy(
            src_ref=whole.at[part(me)],
            dst_ref=whole.at[part(me)],
            send_sem=ag_send.at[d],
            recv_sem=ag_recv.at[d],
            device_id=(lax.rem(me + d, n), ch),
            device_id_type=MESH,
        )

    def ag_arrival(d):
        come = part(lax.rem(me + n - d, n))
        return pltpu.make_async_remote_copy(
            src_ref=whole.at[come],
            dst_ref=whole.at[come],
            send_sem=ag_send.at[d],
            recv_sem=ag_recv.at[d],
            device_id=(lax.rem(me + d, n), ch),
            device_id_type=MESH,
        )

    def each(act):
        def step(d, carry):
            act(d)
            return carry

        lax.fori_loop(1, n, step, 0)

    each(lambda d: rs_copy(d).start())

    @pl.when(jnp.logical_not(last))
    def _():
        for f in (1, 0):
            g_halo(f).wait_recv()
            g_relay(f).start()

    g_share(1).wait_recv()
    g_share(0).wait_recv()
    v_mine = v_own[:, pl.ds(half, own), :].reshape(taps, 2 * full)
    y[0] = dot(v_mine, ge[0 : 2 * full, :])
    y[1] = dot(v_mine[:, 0:full], ge[full : 2 * full, :])

    def add_part(d, total):
        rs_copy(d).wait_recv()
        return total + parts[d].astype(F32)

    total = lax.fori_loop(1, n, add_part, pack[part(me), :].astype(F32))
    whole[part(me), :] = total.astype(BF16)
    each(lambda d: ag_copy(d).start())

    @pl.when(jnp.logical_not(last))
    def _():
        for f in (1, 0):
            g_relay(f).wait_recv()

    v_other = v_late[:, pl.ds(half, own), :].reshape(taps, 2 * full)
    v_first = jnp.concatenate(
        [v_late[t, pl.ds(half, own), full : 2 * full] for t in range(9)], 0
    )
    y[0] += dot(v_first, ge[2 * full : 3 * full, :])
    y[1] += dot(v_other, ge[2 * full : 4 * full, :])
    for f in range(2):
        for block in range(0, own, 16):
            gin_ref[f, block : block + 16, :] = spatial_sum(f, block, 16, -1).astype(BF16)

    each(lambda d: ag_arrival(d).wait_recv())
    top = whole[0:taps, :].astype(F32) * norm
    mid = whole[taps:base, :].astype(F32) * norm
    tail = jnp.concatenate(
        [
            whole[base : base + min(taps, (k + 1) * piece) - k * piece, :].astype(F32)[
                :, rest * k : rest * (k + 1)
            ]
            for k in range(4)
        ],
        0,
    ) * norm
    gw_ref[0:9, :, :] = top[:, 0:full].reshape(9, own, full)
    gw_ref[9:18, :, 0 : 128 - full] = top[:, full:128].reshape(9, own, 128 - full)
    gw_ref[9:18, :, 128 - full : full] = mid[:, 0 : 2 * full - 128].reshape(9, own, 2 * full - 128)
    gw_ref[18:27, :, 0 : 256 - 2 * full] = mid[:, 2 * full - 128 : 128].reshape(
        9, own, 256 - 2 * full
    )
    gw_ref[18:27, :, 256 - 2 * full : full] = tail.reshape(9, own, rest)
    ones = jnp.ones((8, 128), BF16)
    gb_ref[...] = dot_nt(ones, whole[base + piece : base + piece + own, :])[0:1, :] * norm

    for f in range(2):
        x_share(f).wait_send()
        g_share(f).wait_send()

    @pl.when(jnp.logical_not(last))
    def _():
        for f in range(2):
            x_halo(f).wait_send()
            g_relay(f).wait_send()

    @pl.when(jnp.logical_not(first))
    def _():
        for f in range(2):
            g_halo(f).wait_send()
            x_relay(f).wait_send()

    each(lambda d: rs_copy(d).wait_send())
    each(lambda d: ag_copy(d).wait_send())


def local(latents, weight, conv_bias, cotangent):
    own, frames, pix = latents.shape
    n = lax.axis_size("tm")
    full = weight.shape[1]
    norm = 1.0 / math.sqrt(frames * n * pix)
    need = 2 * 9 * own + 112 + own
    chunk = -(-need // (16 * n)) * 16
    vmem = pl.BlockSpec(memory_space=pltpu.VMEM)
    dma = pltpu.SemaphoreType.DMA
    out, gin, gw, gb = pl.pallas_call(
        functools.partial(kernel, n, None, norm),
        out_shape=(
            jax.ShapeDtypeStruct((frames, own, pix), BF16),
            jax.ShapeDtypeStruct((frames, own, pix), BF16),
            jax.ShapeDtypeStruct((27, own, full), F32),
            jax.ShapeDtypeStruct((1, own), F32),
        ),
        in_specs=[vmem] * 4,
        out_specs=(vmem,) * 4,
        scratch_shapes=[
            pltpu.VMEM((4 * full, pix), BF16),
            pltpu.VMEM((4 * full, pix), BF16),
            pltpu.VMEM((9 * own, 2 * full), BF16),
            pltpu.VMEM((9 * own, 2 * full), BF16),
            pltpu.VMEM((9, full, 2 * full), BF16),
            pltpu.VMEM((9, full, 2 * full), BF16),
            pltpu.VMEM((2, 9 * own, pix), F32),
            pltpu.VMEM((2, 9 * own, pix), BF16),
            pltpu.VMEM((n * chunk, 128), BF16),
            pltpu.VMEM((n, chunk, 128), BF16),
            pltpu.VMEM((n * chunk, 128), BF16),
            dma((6,)), dma((6,)), dma((6,)), dma((6,)),
            dma((n,)), dma((n,)), dma((n,)), dma((n,)),
        ],
        compiler_params=pltpu.CompilerParams(
            collective_id=0, has_side_effects=True, vmem_limit_bytes=48 * 1024 * 1024
        ),
    )(
        latents.transpose(1, 0, 2),
        weight,
        conv_bias.reshape(own, 1),
        cotangent.transpose(1, 0, 2),
    )
    return out.transpose(1, 0, 2), gin.transpose(1, 0, 2), gw, gb.reshape(own)


def solution(mesh):
    in_specs = (P("chan", "tm", None), P(), P("chan"), P("chan", "tm", None))
    out_specs = (P("chan", "tm", None), P("chan", "tm", None), P(None, "chan", None), P("chan"))
    return jax.shard_map(local, mesh=mesh, in_specs=in_specs, out_specs=out_specs, check_vma=False)
```

```python
import functools
import math

import jax
import jax.numpy as jnp
from jax import lax
from jax.experimental import pallas as pl
from jax.experimental.pallas import tpu as pltpu
from jax.sharding import PartitionSpec as P

HGT = 8
WID = 112
MESH = pl.DeviceIdType.MESH
F32 = jnp.float32
BF16 = jnp.bfloat16


def dot(a, b):
    return jnp.dot(a, b, preferred_element_type=F32)


def dot_nt(a, b):
    return lax.dot_general(a, b, (((1,), (1,)), ((), ())), preferred_element_type=F32)


def border_masks(pix):
    place = lax.broadcasted_iota(jnp.int32, (1, pix), 1)
    row = jnp.zeros((1, pix), jnp.int32)
    for k in range(1, HGT):
        row = row + (place >= k * WID).astype(jnp.int32)
    col = place - row * WID
    return (
        (row >= 1).astype(F32),
        (row <= HGT - 2).astype(F32),
        (col >= 1).astype(F32),
        (col <= WID - 2).astype(F32),
    )


def kernel(
    n,
    x_ref, w_ref, b_ref, cot_ref,
    out_ref, gin_ref, whole,
    xe, ge, w_early, w_own, v_own, v_late, y, g9, pack, parts,
    x_send, x_recv, g_send, g_recv, rs_send, rs_recv, ag_send, ag_recv,
):
    own = x_ref.shape[1]
    pix = x_ref.shape[2]
    full = 2 * own
    chunk = pack.shape[0] // n
    me = lax.axis_index("tm")
    ch = lax.axis_index("chan")
    other = 1 - ch
    half = pl.multiple_of(ch * own, 16)
    nxt = lax.rem(me + 1, n)
    prv = lax.rem(me + n - 1, n)

    barrier = pltpu.get_barrier_semaphore()

    def greet(d, carry):
        pl.semaphore_signal(
            barrier, inc=1, device_id=(lax.rem(me + d, n), ch), device_id_type=MESH
        )
        return carry

    pl.semaphore_signal(barrier, inc=1, device_id=(me, other), device_id_type=MESH)
    lax.fori_loop(1, n, greet, 0)

    def rows(frame):
        return pl.ds(pl.multiple_of(frame * full + ch * own, 16), own)

    def copy(buf, src, dst, sems, k, device):
        return pltpu.make_async_remote_copy(
            src_ref=buf.at[rows(src)],
            dst_ref=buf.at[rows(dst)],
            send_sem=sems[0].at[k],
            recv_sem=sems[1].at[k],
            device_id=device,
            device_id_type=MESH,
        )

    xs, gs = (x_send, x_recv), (g_send, g_recv)
    for f in range(2):
        xe[rows(2 + f), :] = x_ref[f]

    for tap in range(9):
        to = pl.ds(tap * own, own)
        w0, w1, w2 = (w_ref[9 * t + tap, pl.ds(half, own), :] for t in range(3))
        w_early[to, 0:full] = w0
        w_early[to, full : 2 * full] = w1
        w_own[to, 0:full] = w1
        w_own[to, full : 2 * full] = w2
        v0, v1, v2 = (w_ref[9 * t + tap].T for t in range(3))
        v_own[tap, :, 0:full] = v2
        v_own[tap, :, full : 2 * full] = v1
        v_late[tap, :, 0:full] = v1
        v_late[tap, :, full : 2 * full] = v0

    pl.semaphore_wait(barrier, n)

    def x_share(f):
        return copy(xe, 2 + f, 2 + f, xs, f, (me, other))

    def x_halo(f):
        return copy(xe, 2 + f, f, xs, 2 + f, (nxt, ch))

    def x_relay(f):
        return copy(xe, f, f, xs, 4 + f, (me, other))

    def g_share(f):
        return copy(ge, f, f, gs, f, (me, other))

    def g_halo(f):
        return copy(ge, f, 2 + f, gs, 2 + f, (prv, ch))

    def g_relay(f):
        return copy(ge, 2 + f, 2 + f, gs, 4 + f, (me, other))

    first, last = me == 0, me == n - 1

    @pl.when(jnp.logical_not(last))
    def _():
        x_halo(1).start()
        x_halo(0).start()

    x_share(0).start()
    x_share(1).start()

    @pl.when(first)
    def _():
        xe[0 : 2 * full, :] = jnp.zeros((2 * full, pix), BF16)

    @pl.when(last)
    def _():
        ge[2 * full : 4 * full, :] = jnp.zeros((2 * full, pix), BF16)

    above, below, left, right = border_masks(pix)

    def spatial_sum(f, block, height, sign):
        def at(kh, kw):
            if sign < 0:
                kh, kw = 2 - kh, 2 - kw
            return y[f, pl.ds((3 * kh + kw) * own + block, height), :]

        z = []
        for kw in range(3):
            z.append(
                at(1, kw)
                + above * pltpu.roll(at(0, kw), WID, 1)
                + below * pltpu.roll(at(2, kw), pix - WID, 1)
            )
        return z[1] + left * pltpu.roll(z[0], 1, 1) + right * pltpu.roll(z[2], pix - 1, 1)

    eye = lax.broadcasted_iota(jnp.int32, (own, own), 0) == lax.broadcasted_iota(
        jnp.int32, (own, own), 1
    )
    spread = jnp.where(eye, jnp.broadcast_to(b_ref[...].astype(F32), (own, own)), 0.0)
    bias = dot(spread.astype(BF16), jnp.ones((own, 128), BF16))

    x_share(0).wait_recv()
    x_share(1).wait_recv()
    taps = 9 * own
    w_last = jnp.concatenate([w_ref[18 + t, pl.ds(half, own), :] for t in range(9)], 0)
    y[0] = dot(w_last, xe[2 * full : 3 * full, :])
    y[1] = dot(w_own[...], xe[2 * full : 4 * full, :])

    def x_forward(f):
        @pl.when(jnp.logical_not(first))
        def _():
            x_halo(f).wait_recv()
            x_relay(f).start()

    def x_arrived(f):
        @pl.when(jnp.logical_not(first))
        def _():
            x_relay(f).wait_recv()

    def activate(f, between):
        sums = []
        for block in range(0, own, 16):
            if block == own - 16:
                between()
            pre = spatial_sum(f, block, 16, 1) + bias[block : block + 16, 0:1]
            sig = jax.nn.sigmoid(pre)
            out_ref[f, block : block + 16, :] = (pre * sig).astype(BF16)
            cot = cot_ref[f, block : block + 16, :].astype(F32)
            grad = (cot * sig * (1.0 + pre * (1.0 - sig))).astype(BF16)
            ge[pl.ds(pl.multiple_of(f * full + ch * own + block, 16), 16), :] = grad
            grad = grad.astype(F32)
            sums.append(jnp.sum(grad, axis=1, keepdims=True))
            moved = (
                right * pltpu.roll(grad, pix - 1, 1),
                grad,
                left * pltpu.roll(grad, 1, 1),
            )
            for kw in range(3):
                shifted = (
                    below * pltpu.roll(moved[kw], pix - WID, 1),
                    moved[kw],
                    above * pltpu.roll(moved[kw], WID, 1),
                )
                for kh in range(3):
                    g9[f, pl.ds((3 * kh + kw) * own + block, 16), :] = shifted[kh].astype(BF16)
        g_share(f).start()

        @pl.when(jnp.logical_not(first))
        def _():
            g_halo(f).start()

        return jnp.concatenate(sums, 0)

    x_forward(1)
    x_arrived(1)
    y[1] += dot(w_early[:, 0:full], xe[full : 2 * full, :])
    bias_sum = activate(1, lambda: x_forward(0))
    product = dot_nt(g9[1], xe[full : 4 * full, :])
    x_arrived(0)
    y[0] += dot(w_early[...], xe[0 : 2 * full, :])
    bias_sum += activate(0, lambda: None)

    rest = 3 * full - 256
    piece = 112
    base = 2 * taps
    product += dot_nt(g9[0], xe[0 : 3 * full, :])
    pack[0:taps, :] = product[:, 0:128].astype(BF16)
    pack[taps:base, :] = product[:, 128:256].astype(BF16)
    if pack.shape[0] > base:
        pack[base:, :] = jnp.zeros((pack.shape[0] - base, 128), BF16)
    for k in range(4):
        stop = min(taps, (k + 1) * piece)
        pack[base : base + stop - k * piece, rest * k : rest * (k + 1)] = product[
            k * piece : stop, 256 : 256 + rest
        ].astype(BF16)
    lane = lax.broadcasted_iota(jnp.int32, (own, 128), 1)
    pack[base + piece : base + piece + own, :] = jnp.where(
        lane == 0, jnp.broadcast_to(bias_sum, (own, 128)), 0.0
    ).astype(BF16)

    def part(i):
        return pl.ds(pl.multiple_of(i * chunk, 16), chunk)

    def rs_copy(d):
        to = lax.rem(me + d, n)
        return pltpu.make_async_remote_copy(
            src_ref=pack.at[part(to)],
            dst_ref=parts.at[d],
            send_sem=rs_send.at[d],
            recv_sem=rs_recv.at[d],
            device_id=(to, ch),
            device_id_type=MESH,
        )

    def ag_copy(d):
        return pltpu.make_async_remote_copy(
            src_ref=whole.at[part(me)],
            dst_ref=whole.at[part(me)],
            send_sem=ag_send.at[d],
            recv_sem=ag_recv.at[d],
            device_id=(lax.rem(me + d, n), ch),
            device_id_type=MESH,
        )

    def ag_arrival(d):
        come = part(lax.rem(me + n - d, n))
        return pltpu.make_async_remote_copy(
            src_ref=whole.at[come],
            dst_ref=whole.at[come],
            send_sem=ag_send.at[d],
            recv_sem=ag_recv.at[d],
            device_id=(lax.rem(me + d, n), ch),
            device_id_type=MESH,
        )

    def each(act):
        def step(d, carry):
            act(d)
            return carry

        lax.fori_loop(1, n, step, 0)

    each(lambda d: rs_copy(d).start())

    g_share(1).wait_recv()
    g_share(0).wait_recv()
    v_mine = v_own[:, pl.ds(half, own), :].reshape(taps, 2 * full)
    y[0] = dot(v_mine, ge[0 : 2 * full, :])
    y[1] = dot(v_mine[:, 0:full], ge[full : 2 * full, :])

    @pl.when(jnp.logical_not(last))
    def _():
        for f in (1, 0):
            g_halo(f).wait_recv()
            g_relay(f).start()

    def add_part(d, total):
        rs_copy(d).wait_recv()
        return total + parts[d].astype(F32)

    total = lax.fori_loop(1, n, add_part, pack[part(me), :].astype(F32))
    whole[part(me), :] = total.astype(BF16)
    each(lambda d: ag_copy(d).start())

    @pl.when(jnp.logical_not(last))
    def _():
        for f in (1, 0):
            g_relay(f).wait_recv()

    v_other = v_late[:, pl.ds(half, own), :].reshape(taps, 2 * full)
    v_first = jnp.concatenate(
        [v_late[t, pl.ds(half, own), full : 2 * full] for t in range(9)], 0
    )
    y[0] += dot(v_first, ge[2 * full : 3 * full, :])
    y[1] += dot(v_other, ge[2 * full : 4 * full, :])
    for f in range(2):
        for block in range(0, own, 16):
            gin_ref[f, block : block + 16, :] = spatial_sum(f, block, 16, -1).astype(BF16)

    each(lambda d: ag_arrival(d).wait_recv())
    for f in range(2):
        x_share(f).wait_send()
        g_share(f).wait_send()

    @pl.when(jnp.logical_not(last))
    def _():
        for f in range(2):
            x_halo(f).wait_send()
            g_relay(f).wait_send()

    @pl.when(jnp.logical_not(first))
    def _():
        for f in range(2):
            g_halo(f).wait_send()
            x_relay(f).wait_send()

    each(lambda d: rs_copy(d).wait_send())
    each(lambda d: ag_copy(d).wait_send())


def unpack(norm, own, full, whole, gw_ref, gb_ref):
    taps = 9 * own
    rest = 3 * full - 256
    piece = 112
    base = 2 * taps
    top = whole[0:taps, :].astype(F32) * norm
    mid = whole[taps:base, :].astype(F32) * norm
    tail = jnp.concatenate(
        [
            whole[base : base + min(taps, (k + 1) * piece) - k * piece, :].astype(F32)[
                :, rest * k : rest * (k + 1)
            ]
            for k in range(4)
        ],
        0,
    ) * norm
    gw_ref[0:9, :, :] = top[:, 0:full].reshape(9, own, full)
    gw_ref[9:18, :, 0 : 128 - full] = top[:, full:128].reshape(9, own, 128 - full)
    gw_ref[9:18, :, 128 - full : full] = mid[:, 0 : 2 * full - 128].reshape(9, own, 2 * full - 128)
    gw_ref[18:27, :, 0 : 256 - 2 * full] = mid[:, 2 * full - 128 : 128].reshape(
        9, own, 256 - 2 * full
    )
    gw_ref[18:27, :, 256 - 2 * full : full] = tail.reshape(9, own, rest)
    ones = jnp.ones((8, 128), BF16)
    gb_ref[...] = dot_nt(ones, whole[base + piece : base + piece + own, :])[0:1, :] * norm


def local(latents, weight, conv_bias, cotangent):
    own, frames, pix = latents.shape
    n = lax.axis_size("tm")
    full = weight.shape[1]
    norm = 1.0 / math.sqrt(frames * n * pix)
    need = 2 * 9 * own + 112 + own
    chunk = -(-need // (16 * n)) * 16
    vmem = pl.BlockSpec(memory_space=pltpu.VMEM)
    dma = pltpu.SemaphoreType.DMA
    out, gin, packed = pl.pallas_call(
        functools.partial(kernel, n),
        out_shape=(
            jax.ShapeDtypeStruct((frames, own, pix), BF16),
            jax.ShapeDtypeStruct((frames, own, pix), BF16),
            jax.ShapeDtypeStruct((n * chunk, 128), BF16),
        ),
        in_specs=[vmem] * 4,
        out_specs=(vmem,) * 3,
        scratch_shapes=[
            pltpu.VMEM((4 * full, pix), BF16),
            pltpu.VMEM((4 * full, pix), BF16),
            pltpu.VMEM((9 * own, 2 * full), BF16),
            pltpu.VMEM((9 * own, 2 * full), BF16),
            pltpu.VMEM((9, full, 2 * full), BF16),
            pltpu.VMEM((9, full, 2 * full), BF16),
            pltpu.VMEM((2, 9 * own, pix), F32),
            pltpu.VMEM((2, 9 * own, pix), BF16),
            pltpu.VMEM((n * chunk, 128), BF16),
            pltpu.VMEM((n, chunk, 128), BF16),
            dma((6,)), dma((6,)), dma((6,)), dma((6,)),
            dma((n,)), dma((n,)), dma((n,)), dma((n,)),
        ],
        compiler_params=pltpu.CompilerParams(
            collective_id=0, has_side_effects=True, vmem_limit_bytes=48 * 1024 * 1024
        ),
    )(
        latents.transpose(1, 0, 2),
        weight,
        conv_bias.reshape(1, own),
        cotangent.transpose(1, 0, 2),
    )
    gw, gb = pl.pallas_call(
        functools.partial(unpack, norm, own, full),
        out_shape=(
            jax.ShapeDtypeStruct((27, own, full), F32),
            jax.ShapeDtypeStruct((1, own), F32),
        ),
        in_specs=[vmem],
        out_specs=(vmem,) * 2,
        compiler_params=pltpu.CompilerParams(vmem_limit_bytes=32 * 1024 * 1024),
    )(packed)
    return out.transpose(1, 0, 2), gin.transpose(1, 0, 2), gw, gb.reshape(own)


def solution(mesh):
    in_specs = (P("chan", "tm", None), P(), P("chan"), P("chan", "tm", None))
    out_specs = (P("chan", "tm", None), P("chan", "tm", None), P(None, "chan", None), P("chan"))
    return jax.shard_map(local, mesh=mesh, in_specs=in_specs, out_specs=out_specs, check_vma=False)
```

```python
import functools
import math

import jax
import jax.numpy as jnp
from jax import lax
from jax.experimental import pallas as pl
from jax.experimental.pallas import tpu as pltpu
from jax.sharding import PartitionSpec as P

HGT = 8
WID = 112
MESH = pl.DeviceIdType.MESH
F32 = jnp.float32
BF16 = jnp.bfloat16


def dot(a, b):
    return jnp.dot(a, b, preferred_element_type=F32)


def dot_nt(a, b):
    return lax.dot_general(a, b, (((1,), (1,)), ((), ())), preferred_element_type=F32)


def border_masks(pix):
    place = lax.broadcasted_iota(jnp.int32, (1, pix), 1)
    row = jnp.zeros((1, pix), jnp.int32)
    for k in range(1, HGT):
        row = row + (place >= k * WID).astype(jnp.int32)
    col = place - row * WID
    return (
        (row >= 1).astype(F32),
        (row <= HGT - 2).astype(F32),
        (col >= 1).astype(F32),
        (col <= WID - 2).astype(F32),
    )


def kernel(
    n,
    x_ref, w_ref, b_ref, cot_ref,
    out_ref, gin_ref, whole,
    xe, ge, w_early, w_own, v_own, v_late, y, g9, pack, parts,
    x_send, x_recv, g_send, g_recv, rs_send, rs_recv, ag_send, ag_recv,
):
    own = x_ref.shape[1]
    pix = x_ref.shape[2]
    full = 2 * own
    chunk = pack.shape[0] // n
    half_chunk = chunk // 2
    me = lax.axis_index("tm")
    ch = lax.axis_index("chan")
    other = 1 - ch
    half = pl.multiple_of(ch * own, 16)
    nxt = lax.rem(me + 1, n)
    prv = lax.rem(me + n - 1, n)

    barrier = pltpu.get_barrier_semaphore()

    def greet(d, carry):
        pl.semaphore_signal(
            barrier, inc=1, device_id=(lax.rem(me + d, n), ch), device_id_type=MESH
        )
        return carry

    pl.semaphore_signal(barrier, inc=1, device_id=(me, other), device_id_type=MESH)
    lax.fori_loop(1, n, greet, 0)

    def rows(frame):
        return pl.ds(pl.multiple_of(frame * full + ch * own, 16), own)

    def copy(buf, src, dst, sems, k, device):
        return pltpu.make_async_remote_copy(
            src_ref=buf.at[rows(src)],
            dst_ref=buf.at[rows(dst)],
            send_sem=sems[0].at[k],
            recv_sem=sems[1].at[k],
            device_id=device,
            device_id_type=MESH,
        )

    xs, gs = (x_send, x_recv), (g_send, g_recv)
    for f in range(2):
        xe[rows(2 + f), :] = x_ref[f]

    for tap in range(9):
        to = pl.ds(tap * own, own)
        w0, w1, w2 = (w_ref[9 * t + tap, pl.ds(half, own), :] for t in range(3))
        w_early[to, 0:full] = w0
        w_early[to, full : 2 * full] = w1
        w_own[to, 0:full] = w1
        w_own[to, full : 2 * full] = w2
        v0, v1, v2 = (w_ref[9 * t + tap].T for t in range(3))
        v_own[tap, :, 0:full] = v2
        v_own[tap, :, full : 2 * full] = v1
        v_late[tap, :, 0:full] = v1
        v_late[tap, :, full : 2 * full] = v0

    pl.semaphore_wait(barrier, n)

    def x_share(f):
        return copy(xe, 2 + f, 2 + f, xs, f, (me, other))

    def x_halo(f):
        return copy(xe, 2 + f, f, xs, 2 + f, (nxt, ch))

    def x_relay(f):
        return copy(xe, f, f, xs, 4 + f, (me, other))

    def g_share(f):
        return copy(ge, f, f, gs, f, (me, other))

    def g_halo(f):
        return copy(ge, f, 2 + f, gs, 2 + f, (prv, ch))

    def g_relay(f):
        return copy(ge, 2 + f, 2 + f, gs, 4 + f, (me, other))

    first, last = me == 0, me == n - 1

    @pl.when(jnp.logical_not(last))
    def _():
        x_halo(1).start()
        x_halo(0).start()

    x_share(0).start()
    x_share(1).start()

    @pl.when(first)
    def _():
        xe[0 : 2 * full, :] = jnp.zeros((2 * full, pix), BF16)

    @pl.when(last)
    def _():
        ge[2 * full : 4 * full, :] = jnp.zeros((2 * full, pix), BF16)

    above, below, left, right = border_masks(pix)

    def spatial_sum(f, block, height, sign):
        def at(kh, kw):
            if sign < 0:
                kh, kw = 2 - kh, 2 - kw
            return y[f, pl.ds((3 * kh + kw) * own + block, height), :]

        z = []
        for kw in range(3):
            z.append(
                at(1, kw)
                + above * pltpu.roll(at(0, kw), WID, 1)
                + below * pltpu.roll(at(2, kw), pix - WID, 1)
            )
        return z[1] + left * pltpu.roll(z[0], 1, 1) + right * pltpu.roll(z[2], pix - 1, 1)

    eye = lax.broadcasted_iota(jnp.int32, (own, own), 0) == lax.broadcasted_iota(
        jnp.int32, (own, own), 1
    )
    spread = jnp.where(eye, jnp.broadcast_to(b_ref[...].astype(F32), (own, own)), 0.0)
    bias = dot(spread.astype(BF16), jnp.ones((own, 128), BF16))

    x_share(0).wait_recv()
    x_share(1).wait_recv()
    taps = 9 * own
    w_last = jnp.concatenate([w_ref[18 + t, pl.ds(half, own), :] for t in range(9)], 0)
    y[0] = dot(w_last, xe[2 * full : 3 * full, :])
    y[1] = dot(w_own[...], xe[2 * full : 4 * full, :])

    def x_forward(f):
        @pl.when(jnp.logical_not(first))
        def _():
            x_halo(f).wait_recv()
            x_relay(f).start()

    def x_arrived(f):
        @pl.when(jnp.logical_not(first))
        def _():
            x_relay(f).wait_recv()

    def activate(f, between):
        sums = []
        for block in range(0, own, 16):
            if block == own - 16:
                between()
            pre = spatial_sum(f, block, 16, 1) + bias[block : block + 16, 0:1]
            sig = jax.nn.sigmoid(pre)
            out_ref[f, block : block + 16, :] = (pre * sig).astype(BF16)
            cot = cot_ref[f, block : block + 16, :].astype(F32)
            grad = (cot * sig * (1.0 + pre * (1.0 - sig))).astype(BF16)
            ge[pl.ds(pl.multiple_of(f * full + ch * own + block, 16), 16), :] = grad
            grad = grad.astype(F32)
            sums.append(jnp.sum(grad, axis=1, keepdims=True))
            moved = (
                right * pltpu.roll(grad, pix - 1, 1),
                grad,
                left * pltpu.roll(grad, 1, 1),
            )
            for kw in range(3):
                shifted = (
                    below * pltpu.roll(moved[kw], pix - WID, 1),
                    moved[kw],
                    above * pltpu.roll(moved[kw], WID, 1),
                )
                for kh in range(3):
                    g9[f, pl.ds((3 * kh + kw) * own + block, 16), :] = shifted[kh].astype(BF16)
        g_share(f).start()

        @pl.when(jnp.logical_not(first))
        def _():
            g_halo(f).start()

        return jnp.concatenate(sums, 0)

    x_forward(1)
    x_arrived(1)
    y[1] += dot(w_early[:, 0:full], xe[full : 2 * full, :])
    bias_sum = activate(1, lambda: x_forward(0))
    product_late = dot_nt(g9[1], xe[full : 4 * full, :])
    x_arrived(0)
    y[0] += dot(w_early[...], xe[0 : 2 * full, :])
    bias_sum += activate(0, lambda: None)

    rest = 3 * full - 256
    piece = 112
    base = 2 * taps
    middle = n * chunk // 2

    def part(h, i):
        return pl.ds(pl.multiple_of(h * middle + i * half_chunk, 16), half_chunk)

    def rs_copy(h, d):
        to = lax.rem(me + d, n)
        return pltpu.make_async_remote_copy(
            src_ref=pack.at[part(h, to)],
            dst_ref=parts.at[h, d],
            send_sem=rs_send.at[h, d],
            recv_sem=rs_recv.at[h, d],
            device_id=(to, ch),
            device_id_type=MESH,
        )

    def ag_copy(h, d):
        return pltpu.make_async_remote_copy(
            src_ref=whole.at[part(h, me)],
            dst_ref=whole.at[part(h, me)],
            send_sem=ag_send.at[h, d],
            recv_sem=ag_recv.at[h, d],
            device_id=(lax.rem(me + d, n), ch),
            device_id_type=MESH,
        )

    def ag_arrival(h, d):
        come = part(h, lax.rem(me + n - d, n))
        return pltpu.make_async_remote_copy(
            src_ref=whole.at[come],
            dst_ref=whole.at[come],
            send_sem=ag_send.at[h, d],
            recv_sem=ag_recv.at[h, d],
            device_id=(lax.rem(me + d, n), ch),
            device_id_type=MESH,
        )

    def each(act):
        def step(d, carry):
            act(d)
            return carry

        lax.fori_loop(1, n, step, 0)

    wide = product_late[:, 0:256] + dot_nt(g9[0], xe[0:256, :])
    pack[0:taps, :] = wide[:, 0:128].astype(BF16)
    pack[taps:base, :] = wide[:, 128:256].astype(BF16)
    early_start = middle <= base
    if early_start:
        each(lambda d: rs_copy(0, d).start())
    narrow = product_late[:, 256:] + dot_nt(g9[0], xe[256 : 3 * full, :])
    pack[base:, :] = jnp.zeros((pack.shape[0] - base, 128), BF16)
    for k in range(4):
        stop = min(taps, (k + 1) * piece)
        pack[base : base + stop - k * piece, rest * k : rest * (k + 1)] = narrow[
            k * piece : stop, :
        ].astype(BF16)
    lane = lax.broadcasted_iota(jnp.int32, (own, 128), 1)
    pack[base + piece : base + piece + own, :] = jnp.where(
        lane == 0, jnp.broadcast_to(bias_sum, (own, 128)), 0.0
    ).astype(BF16)
    if not early_start:
        each(lambda d: rs_copy(0, d).start())
    each(lambda d: rs_copy(1, d).start())

    g_share(1).wait_recv()
    g_share(0).wait_recv()
    v_mine = v_own[:, pl.ds(half, own), :].reshape(taps, 2 * full)
    y[0] = dot(v_mine, ge[0 : 2 * full, :])
    y[1] = dot(v_mine[:, 0:full], ge[full : 2 * full, :])

    @pl.when(jnp.logical_not(last))
    def _():
        for f in (1, 0):
            g_halo(f).wait_recv()
            g_relay(f).start()

    for h in range(2):

        def add_part(d, total):
            rs_copy(h, d).wait_recv()
            return total + parts[h, d].astype(F32)

        total = lax.fori_loop(1, n, add_part, pack[part(h, me), :].astype(F32))
        whole[part(h, me), :] = total.astype(BF16)
        each(lambda d: ag_copy(h, d).start())

    @pl.when(jnp.logical_not(last))
    def _():
        for f in (1, 0):
            g_relay(f).wait_recv()

    v_other = v_late[:, pl.ds(half, own), :].reshape(taps, 2 * full)
    v_first = jnp.concatenate(
        [v_late[t, pl.ds(half, own), full : 2 * full] for t in range(9)], 0
    )
    y[0] += dot(v_first, ge[2 * full : 3 * full, :])
    y[1] += dot(v_other, ge[2 * full : 4 * full, :])
    for f in range(2):
        for block in range(0, own, 16):
            gin_ref[f, block : block + 16, :] = spatial_sum(f, block, 16, -1).astype(BF16)

    for h in range(2):
        each(lambda d: ag_arrival(h, d).wait_recv())
    for f in range(2):
        x_share(f).wait_send()
        g_share(f).wait_send()

    @pl.when(jnp.logical_not(last))
    def _():
        for f in range(2):
            x_halo(f).wait_send()
            g_relay(f).wait_send()

    @pl.when(jnp.logical_not(first))
    def _():
        for f in range(2):
            g_halo(f).wait_send()
            x_relay(f).wait_send()

    for h in range(2):
        each(lambda d: rs_copy(h, d).wait_send())
        each(lambda d: ag_copy(h, d).wait_send())


def unpack(norm, own, full, whole, gw_ref, gb_ref):
    taps = 9 * own
    rest = 3 * full - 256
    piece = 112
    base = 2 * taps
    top = whole[0:taps, :].astype(F32) * norm
    mid = whole[taps:base, :].astype(F32) * norm
    tail = jnp.concatenate(
        [
            whole[base : base + min(taps, (k + 1) * piece) - k * piece, :].astype(F32)[
                :, rest * k : rest * (k + 1)
            ]
            for k in range(4)
        ],
        0,
    ) * norm
    gw_ref[0:9, :, :] = top[:, 0:full].reshape(9, own, full)
    gw_ref[9:18, :, 0 : 128 - full] = top[:, full:128].reshape(9, own, 128 - full)
    gw_ref[9:18, :, 128 - full : full] = mid[:, 0 : 2 * full - 128].reshape(9, own, 2 * full - 128)
    gw_ref[18:27, :, 0 : 256 - 2 * full] = mid[:, 2 * full - 128 : 128].reshape(
        9, own, 256 - 2 * full
    )
    gw_ref[18:27, :, 256 - 2 * full : full] = tail.reshape(9, own, rest)
    ones = jnp.ones((8, 128), BF16)
    gb_ref[...] = dot_nt(ones, whole[base + piece : base + piece + own, :])[0:1, :] * norm


def local(latents, weight, conv_bias, cotangent):
    own, frames, pix = latents.shape
    n = lax.axis_size("tm")
    full = weight.shape[1]
    norm = 1.0 / math.sqrt(frames * n * pix)
    need = 2 * 9 * own + 112 + own
    chunk = -(-need // (32 * n)) * 32
    vmem = pl.BlockSpec(memory_space=pltpu.VMEM)
    dma = pltpu.SemaphoreType.DMA
    out, gin, packed = pl.pallas_call(
        functools.partial(kernel, n),
        out_shape=(
            jax.ShapeDtypeStruct((frames, own, pix), BF16),
            jax.ShapeDtypeStruct((frames, own, pix), BF16),
            jax.ShapeDtypeStruct((n * chunk, 128), BF16),
        ),
        in_specs=[vmem] * 4,
        out_specs=(vmem,) * 3,
        scratch_shapes=[
            pltpu.VMEM((4 * full, pix), BF16),
            pltpu.VMEM((4 * full, pix), BF16),
            pltpu.VMEM((9 * own, 2 * full), BF16),
            pltpu.VMEM((9 * own, 2 * full), BF16),
            pltpu.VMEM((9, full, 2 * full), BF16),
            pltpu.VMEM((9, full, 2 * full), BF16),
            pltpu.VMEM((2, 9 * own, pix), F32),
            pltpu.VMEM((2, 9 * own, pix), BF16),
            pltpu.VMEM((n * chunk, 128), BF16),
            pltpu.VMEM((2, n, chunk // 2, 128), BF16),
            dma((6,)), dma((6,)), dma((6,)), dma((6,)),
            dma((2, n)), dma((2, n)), dma((2, n)), dma((2, n)),
        ],
        compiler_params=pltpu.CompilerParams(
            collective_id=0, has_side_effects=True, vmem_limit_bytes=48 * 1024 * 1024
        ),
    )(
        latents.transpose(1, 0, 2),
        weight,
        conv_bias.reshape(1, own),
        cotangent.transpose(1, 0, 2),
    )
    gw, gb = pl.pallas_call(
        functools.partial(unpack, norm, own, full),
        out_shape=(
            jax.ShapeDtypeStruct((27, own, full), F32),
            jax.ShapeDtypeStruct((1, own), F32),
        ),
        in_specs=[vmem],
        out_specs=(vmem,) * 2,
        compiler_params=pltpu.CompilerParams(vmem_limit_bytes=32 * 1024 * 1024),
    )(packed)
    return out.transpose(1, 0, 2), gin.transpose(1, 0, 2), gw, gb.reshape(own)


def solution(mesh):
    in_specs = (P("chan", "tm", None), P(), P("chan"), P("chan", "tm", None))
    out_specs = (P("chan", "tm", None), P("chan", "tm", None), P(None, "chan", None), P("chan"))
    return jax.shard_map(local, mesh=mesh, in_specs=in_specs, out_specs=out_specs, check_vma=False)
```
